128 devices in a mesh: atom: 16 (over y, z), fit: 8 (over x, core).
Axes of the slice: x: 4, y: 4, z: 4, core: 2. Of those that a mesh axis runs over, the one named last changes fastest.
Arguments:
- three_centre: bfloat16 [192, 4, 384, 4096], P('atom', None, 'fit'), may hold values from -0.375 to 0.375
- tensor_pattern: int32 [192, 4], P('atom'), may hold values from 0 to 191, all different within a row
- coefficients: bfloat16 [32, 12288], P(None, 'atom'), may hold values from -6 to 6
- readers: int32 [192, 4], replicated, may hold values from 0 to 15, all different within a row; in each aligned block of 12 rows (0 to 11, 12 to 23, ...) at most 6 rows name the same one
Outputs:
- exchange_matrix: bfloat16 [12288, 12288], P(('atom', 'fit'))
The draws below stay inside these ranges and needn't reach their ends.
Inputs may be any that keep to these rules, and one draw needn't show every extreme that they name: `tensor_pattern`: each row names 4 different blocks, and every block is named by some row. `readers`: each row names 4 different devices, possibly the block's own. Among the 12 blocks of one device (rows b with equal b // 12), no device is named more than 6 times, and in some of these groups a device is named exactly 6 times.
All inputs are finite; a program needn't handle non-finite values.
Results may differ from the reference program's by a relative error of at most 0.0057.
Values may be sent and summed in bfloat16 or wider, within the bound.
No kernel may reach another device: no remote copies, remote signals or barrier semaphores. Data moves between devices by JAX's collectives and lax.ppermute only.
A program may use at most 192 MiB of HBM per device.

```python
import math
import jax
import jax.numpy as jnp
import numpy as np
from jax import lax

BS = 64
NB_DEV = 12
NOCC = 32
KB = 4
NR = 4
CAP = 6
NB = 192
NBAS = 12288
NPT = 384
SLOTS = 108
N_ATOM = 16


def shard_levels(own_key, dims, pieces, least, largest):
    factor_of = 1.0
    for position, parts in pieces:
        steps = jax.random.uniform(jax.random.fold_in(jax.random.fold_in(own_key, 6), position), (parts,), jnp.float32, least / len(pieces), largest / len(pieces))
        factor_of = factor_of * jnp.repeat(jnp.exp(steps), dims[position] // parts).reshape((-1,) + (1,) * (len(dims) - 1 - position))
    return factor_of


def different_ones(stream_key, rows, amount, top, lift):
    sequence = jax.random.permutation(jax.random.fold_in(stream_key, 1), amount)
    favour = sequence
    for power in range(3):
        favour = favour * favour // amount
    favour = favour * lift // amount
    tickets = jax.random.randint(jax.random.fold_in(stream_key, 2), (rows, amount), 0, 4096) + favour
    holders = jax.random.permutation(jax.random.fold_in(stream_key, 3), rows)[jnp.arange(amount) % rows]
    tickets = jnp.where(jnp.arange(rows)[:, None] == holders[None, :], 1 << 14, tickets)
    priority = tickets * amount + jnp.arange(amount)
    return lax.top_k(priority.astype(jnp.int32), top)[1].astype(jnp.int32)


def deal_out(rng, own, number, rows, amount, top, reach, skew):
    order = jax.random.permutation(rng, amount)
    heavy_load, common = portions_of(amount, rows * top, reach, skew, True), portions_of(amount, rows * top, reach, skew, False)
    places = jnp.arange(amount)

    def named(lengths, turn):
        used = int((lengths > 0).sum())
        fixed = max(1, used // 4)
        shifted = fixed + (places - fixed + turn * (used - fixed)) % max(1, amount - fixed)
        return jnp.zeros((amount,), jnp.int32).at[order[jnp.where(places < fixed, places, shifted)]].set(jnp.asarray(lengths, jnp.int32))

    lengths = jnp.where(number % 4 == 0, named(heavy_load, number // 4), named(common, number - number // 4 - 1))
    mixed = jax.random.permutation(jax.random.fold_in(own, 3), amount)
    giver, taker = mixed[0:amount // 2 * 2:2], mixed[1:amount // 2 * 2:2]
    slack = jnp.minimum(lengths[giver] - 1, reach - lengths[taker]) // 2
    slack = jnp.where((giver == order[0]) | (taker == order[0]) | (lengths[taker] == 0), 0, jnp.maximum(slack, 0))
    shifted = jax.random.randint(jax.random.fold_in(own, 4), (amount // 2,), 0, 1 << 20) % (slack + 1)
    lengths = lengths.at[giver].add(-shifted).at[taker].add(shifted)
    labels = jnp.searchsorted(jnp.cumsum(lengths), jnp.arange(rows * top), side="right").astype(jnp.int32)
    listing = labels.reshape(top, rows).T
    listing = listing[jax.random.permutation(jax.random.fold_in(own, 1), rows)]
    turn = jax.random.randint(jax.random.fold_in(own, 2), (rows, 1), 0, top)
    return jnp.take_along_axis(listing, (jnp.arange(top)[None, :] + turn) % top, axis=1)


def portions_of(amount, total, most, skew, full):
    loads = [(1 << 20) // math.isqrt(grade ** skew) + 1 for grade in range(1, amount + 1)]
    largest = most if full else min(most, max(-(-total // amount), total * loads[0] // sum(loads)))
    least = 1 if total - largest >= amount - 1 else 0
    counts, surplus = [largest] + [least] * (amount - 1), total - largest - least * (amount - 1)
    while surplus > 0:
        candidates = [i for i in range(1, amount) if counts[i] < largest] or [i for i in range(1, amount) if counts[i] < most]
        pool, remaining = sum([loads[i] for i in candidates]), surplus
        for i in candidates:
            extra = min(most - counts[i], max(1, remaining * loads[i] // pool), surplus)
            counts[i] = counts[i] + extra
            surplus = surplus - extra
    return np.array(counts)


def normal_values(own_key, extent, deviation, limit, split=(), kind=jnp.bfloat16):
    gain = shard_levels(own_key, extent, split, -0.22, 0.18) if split else 1.0
    values = jax.random.normal(own_key, extent, jnp.float32) * deviation * gain
    return jnp.minimum(jnp.maximum(values, -limit), limit).astype(kind)


def setup_inputs(seed: int = 0) -> dict:
    splits = jax.random.split(jax.random.key(seed), 5)
    three_centre = normal_values(splits[0], (NB, KB, NPT, BS * BS), (KB * BS) ** -0.5, 0.375, ((0, 16), (2, 8)))
    tensor_pattern = different_ones(splits[1], NB, NB, KB, 0)
    coefficients = normal_values(splits[2], (NOCC, NBAS), 1.0, 6.0, ((1, 16),))
    readers_keys = jax.random.split(jax.random.fold_in(splits[3], 1), NB // NB_DEV)
    readers_turns = jax.random.permutation(jax.random.fold_in(splits[3], 3), NB // NB_DEV)
    readers = jax.vmap(lambda own, number: deal_out(jax.random.fold_in(splits[3], 2), own, number, NB_DEV, N_ATOM, NR, CAP, 2))(readers_keys, readers_turns).reshape((NB, NR))
    return dict(three_centre=three_centre, tensor_pattern=tensor_pattern, coefficients=coefficients, readers=readers)


def reference(three_centre, tensor_pattern, coefficients, readers):
    coeff_float = coefficients.astype(jnp.float32)
    offsets = jnp.arange(BS, dtype=jnp.int32)

    def one_block(block_args):
        tile_rows, partners = block_args
        column_ids = (partners[:, None].astype(jnp.int32) * BS + offsets[None, :]).astype(jnp.int32)
        picked = jnp.take(coeff_float, column_ids.reshape(-1), axis=1).reshape(NOCC, KB, BS)
        tile_float = tile_rows.astype(jnp.float32).reshape(KB, NPT, BS, BS)
        fitted = jnp.einsum('kplu,ikl->upi', tile_float, picked)
        return fitted.astype(jnp.bfloat16).reshape(BS, NPT * NOCC)
    fitted_all = lax.map(one_block, (three_centre, tensor_pattern))
    blocks = jnp.arange(NB, dtype=jnp.int32)
    owner_device = blocks // NB_DEV
    read_by = jnp.any(readers[None, :, :] == jnp.arange(N_ATOM, dtype=jnp.int32)[:, None, None], axis=2)
    scale_factor = 1.0 / math.sqrt(NPT * NOCC)

    def one_group(group_index):
        row_values = lax.dynamic_slice_in_dim(fitted_all, group_index * NB_DEV, NB_DEV, 0)
        row_values = row_values.astype(jnp.float32).reshape(NB_DEV * BS, NPT * NOCC)
        wanted = jnp.logical_or(owner_device == group_index, read_by[group_index])
        chosen = jnp.nonzero(wanted, size=SLOTS, fill_value=0)[0].astype(jnp.int32)
        wanted_count = jnp.sum(wanted.astype(jnp.int32))
        valid_slot = jnp.arange(SLOTS, dtype=jnp.int32) < wanted_count
        column_values = jnp.take(fitted_all, chosen, axis=0).astype(jnp.float32)
        products = jnp.einsum('rf,sbf->rsb', row_values, column_values)
        onehot = jnp.logical_and(chosen[:, None] == blocks[None, :], valid_slot[:, None]).astype(jnp.float32)
        dense_terms = jnp.einsum('rsb,sn->rnb', products, onehot, precision=lax.Precision.HIGHEST)
        row_block = group_index * NB_DEV + jnp.arange(NB_DEV * BS, dtype=jnp.int32) // BS
        keep_mask = (row_block[:, None] != blocks[None, :]).astype(jnp.float32)
        dense_terms = dense_terms * keep_mask[:, :, None]
        return dense_terms.reshape(NB_DEV * BS, NBAS) * scale_factor
    result = lax.map(one_group, jnp.arange(N_ATOM, dtype=jnp.int32))
    return result.reshape(NBAS, NBAS).astype(jnp.bfloat16)
```

```python
import functools
import math

import jax
import jax.numpy as jnp
import numpy as np
from jax import lax
from jax.experimental import pallas as pl
from jax.experimental.pallas import tpu as pltpu
from jax.sharding import PartitionSpec as P

BS = 64
KB = 4
NBD = 12
CAP = 6
NP = 48
NOCC = 32
HALF = NP * NOCC // 2
SIDE = 4
FIT = 8
ROWS = NBD * BS
PIECE = ROWS // FIT
MIB = 2**20

STEP = {"+y": (1, 0), "-y": (3, 0), "+z": (0, 1), "-z": (0, 3)}
PLAN = (
    (1, 1, (1, 0), (0, 0), "+y", True),
    (1, 0, (0, 1), (0, 0), "+z", True),
    (1, 1, (3, 0), (0, 0), "-y", False),
    (1, 0, (3, 0), (0, 0), "-y", False),
    (1, 0, (0, 3), (0, 0), "-z", True),
    (2, 0, (1, 1), (0, 1), "+y", True),
    (2, 1, (1, 1), (1, 0), "+z", True),
    (2, 0, (3, 3), (0, 3), "-y", True),
    (2, 1, (0, 3), (0, 0), "-z", True),
    (3, 0, (1, 3), (0, 3), "+y", False),
    (3, 0, (1, 0), (0, 0), "+y", False),
    (3, 1, (0, 1), (0, 0), "+z", False),
    (3, 0, (0, 2), (0, 1), "+z", False),
    (3, 1, (3, 3), (0, 3), "-y", True),
    (3, 1, (0, 2), (0, 3), "-z", False),
    (3, 1, (1, 3), (1, 0), "-z", False),
    (4, 1, (2, 1), (1, 1), "+y", True),
    (4, 1, (1, 2), (1, 1), "+z", False),
    (4, 0, (1, 2), (1, 1), "+z", False),
    (4, 0, (2, 3), (3, 3), "-y", True),
    (4, 1, (3, 2), (3, 3), "-z", False),
    (4, 0, (3, 2), (3, 3), "-z", False),
    (5, 0, (2, 1), (1, 1), "+y", False),
    (5, 1, (3, 1), (2, 1), "+y", False),
    (5, 1, (2, 2), (2, 1), "+z", False),
    (5, 0, (2, 0), (2, 3), "+z", False),
    (5, 0, (3, 1), (0, 1), "-y", False),
    (5, 1, (2, 3), (3, 3), "-y", False),
    (5, 0, (2, 2), (2, 3), "-z", False),
    (5, 1, (2, 0), (2, 1), "-z", False),
)
OFFSETS = tuple(
    sorted({p[2] for p in PLAN}, key=lambda o: (max(p[0] for p in PLAN if p[2] == o), o))
)
DONE = {o: max(p[0] for p in PLAN if p[2] == o) for o in OFFSETS}
CHUNKS = (
    tuple(o for o in OFFSETS if DONE[o] <= 3),
    tuple(o for o in OFFSETS if DONE[o] > 3),
)
TILES = CAP // 2
OWN_TILES = NBD // 2
BASE = {(0, 0): 0}
for _o in CHUNKS[0] + CHUNKS[1]:
    BASE[_o] = OWN_TILES + TILES * (len(BASE) - 1)
COUNT = (OWN_TILES + TILES * len(CHUNKS[0]), TILES * len(CHUNKS[1]))


def minus(a, b):
    return ((a[0] - b[0]) % SIDE, (a[1] - b[1]) % SIDE)


def plus(a, b):
    return ((a[0] + b[0]) % SIDE, (a[1] + b[1]) % SIDE)


def number(a):
    return a[0] * SIDE + a[1]


PLACES = tuple((y, z) for y in range(SIDE) for z in range(SIDE))
LEAVES = tuple(p for p in PLAN if not p[5])
PAIRS = np.array(
    [
        [(number(minus(me, o)), number(me)) for o in OFFSETS]
        + [
            (number(minus(plus(me, STEP[p[4]]), p[2])), number(plus(me, STEP[p[4]])))
            for p in LEAVES
        ]
        for me in PLACES
    ],
    dtype=np.int32,
)
BASE_OF = np.array([[BASE[minus(me, h)] for h in PLACES] for me in PLACES], dtype=np.int32)


def fit_kernel(tile_ref, coeff_ref, first_ref, second_ref, lines):
    for m in range(2):
        for k in range(KB):
            for pair in range(BS // 2):
                value = tile_ref[m, k, :, pair * 128 : (pair + 1) * 128]
                lines[m, pl.ds((k * 32 + pair) * NP, NP), :] = value.astype(jnp.float32)
    for group in range(NP // 4):
        both = []
        for m in range(2):
            parts = []
            for p in range(group * 4, group * 4 + 4):
                rows = lines[m, pl.ds(p, 128, stride=NP), :].astype(jnp.bfloat16)
                product = jnp.dot(coeff_ref[m], rows, preferred_element_type=jnp.float32)
                parts.append(product[0:NOCC] + pltpu.roll(product[NOCC:], 64, 1))
            both.append(jnp.concatenate(parts, axis=0)[:, 0:BS])
        turned = jnp.concatenate(both, axis=1).T.astype(jnp.bfloat16)
        out_ref = first_ref if group < 6 else second_ref
        place = (group % 6) * 128
        out_ref[0, :, place : place + 128] = turned[0:BS]
        out_ref[1, :, place : place + 128] = turned[BS:]


def fit_rows(three_centre, picked):
    out = jax.ShapeDtypeStruct((NBD, BS, HALF), jnp.bfloat16)
    return pl.pallas_call(
        fit_kernel,
        grid=(NBD // 2,),
        in_specs=[
            pl.BlockSpec((2, KB, NP, BS * BS), lambda g: (g, 0, 0, 0)),
            pl.BlockSpec((2, 2 * NOCC, 128), lambda g: (g, 0, 0)),
        ],
        out_specs=[pl.BlockSpec((2, BS, HALF), lambda g: (g, 0, 0))] * 2,
        out_shape=[out, out],
        scratch_shapes=[pltpu.VMEM((2, KB * 32 * NP, 128), jnp.float32)],
        compiler_params=pltpu.CompilerParams(vmem_limit_bytes=40 * MIB),
    )(three_centre, picked)


def pack_kernel(index_ref, left_ref, right_ref, out_ref):
    step = pl.program_id(0)

    @pl.when(step < CAP)
    def _():
        out_ref[...] = left_ref[...]

    @pl.when(step >= CAP)
    def _():
        out_ref[...] = right_ref[...]


def pack(left, right, index):
    block = (1, BS, HALF)
    return pl.pallas_call(
        pack_kernel,
        grid_spec=pltpu.PrefetchScalarGridSpec(
            num_scalar_prefetch=1,
            grid=(2 * CAP,),
            in_specs=[
                pl.BlockSpec(block, lambda s, ix: (ix[jnp.minimum(s, CAP - 1)], 0, 0)),
                pl.BlockSpec(block, lambda s, ix: (ix[jnp.maximum(s, CAP)], 0, 0)),
            ],
            out_specs=pl.BlockSpec(block, lambda s, ix: (s, 0, 0)),
        ),
        out_shape=jax.ShapeDtypeStruct((NBD, BS, HALF), jnp.bfloat16),
        compiler_params=pltpu.CompilerParams(vmem_limit_bytes=16 * MIB),
        cost_estimate=pl.CostEstimate(flops=0, bytes_accessed=5 * MIB, transcendentals=0),
    )(index, left, right)


def product_kernel(scale, index_ref, own_a, own_b, far_a, far_b, _, out_ref, side_a, side_b):
    @pl.when(pl.program_id(0) == 0)
    def _():
        for s in range(CAP):
            side_a[s * BS : (s + 1) * BS, :] = far_a[index_ref[s]]
            side_b[s * BS : (s + 1) * BS, :] = far_b[index_ref[CAP + s]]

    last = (((1,), (1,)), ((), ()))
    total = lax.dot_general(own_a[...], side_a[...], last, preferred_element_type=jnp.float32)
    total += lax.dot_general(own_b[...], side_b[...], last, preferred_element_type=jnp.float32)
    total = (total * scale).astype(jnp.bfloat16)
    for f in range(FIT // 2):
        for t in range(TILES):
            out_ref[f, t] = total[f * PIECE : (f + 1) * PIECE, t * 128 : (t + 1) * 128]


def product(own, far, index, buffer, tile, count, scale):
    whole = pl.BlockSpec((NBD, BS, HALF), lambda m, ix: (0, 0, 0))
    rows = pl.BlockSpec((ROWS // 2, HALF), lambda m, ix: (m, 0))
    shape = jax.ShapeDtypeStruct((FIT, count, PIECE, 128), jnp.bfloat16)
    if buffer is None:
        given, aliases = [], {}
    else:
        given, aliases = [buffer], {5: 0}
    kernel = functools.partial(product_kernel, scale)
    if buffer is None:
        inner = kernel
        kernel = lambda ix, a, b, c, d, *rest: inner(ix, a, b, c, d, None, *rest)
    return pl.pallas_call(
        kernel,
        grid_spec=pltpu.PrefetchScalarGridSpec(
            num_scalar_prefetch=1,
            grid=(2,),
            in_specs=[rows, rows, whole, whole] + [pl.BlockSpec(memory_space=pl.ANY)] * len(given),
            out_specs=pl.BlockSpec(
                (FIT // 2, TILES, PIECE, 128), lambda m, ix: (m, tile // TILES, 0, 0)
            ),
            scratch_shapes=[pltpu.VMEM((CAP * BS, HALF), jnp.bfloat16)] * 2,
        ),
        out_shape=shape,
        input_output_aliases=aliases,
        compiler_params=pltpu.CompilerParams(vmem_limit_bytes=24 * MIB),
        cost_estimate=pl.CostEstimate(
            flops=2 * ROWS * CAP * BS * 2 * HALF, bytes_accessed=6 * MIB, transcendentals=0
        ),
    )(index, own[0].reshape(ROWS, HALF), own[1].reshape(ROWS, HALF), far[0], far[1], *given)


def place_kernel(source_ref, here_ref, first_ref, second_ref, out_ref):
    lane = lax.broadcasted_iota(jnp.int32, (PIECE, 128), 1)
    line = lax.broadcasted_iota(jnp.int32, (PIECE, 128), 0)
    row_block = here_ref[0] * NBD + ((line + here_ref[1] * PIECE) >> 6)

    def fetch(slot):
        tile = jnp.maximum(slot, 0) >> 1
        near = first_ref[0, jnp.minimum(tile, COUNT[0] - 1)]
        far = second_ref[0, jnp.clip(tile - COUNT[0], 0, COUNT[1] - 1)]
        return jnp.where(tile < COUNT[0], near, far).astype(jnp.float32)

    def one(pair, _):
        left, right = source_ref[2 * pair], source_ref[2 * pair + 1]
        a, b = fetch(left), fetch(right)
        a = jnp.where((left & 1) == 1, pltpu.roll(a, 64, 1), a)
        b = jnp.where((right & 1) == 0, pltpu.roll(b, 64, 1), b)
        a = jnp.where(left < 0, 0.0, a)
        b = jnp.where(right < 0, 0.0, b)
        value = jnp.where(lane < 64, a, b)
        block = 2 * pair + (lane >> 6)
        value = jnp.where(row_block == block, 0.0, value)
        out_ref[:, pl.ds(pl.multiple_of(pair * 128, 128), 128)] = value.astype(jnp.bfloat16)
        return 0

    lax.fori_loop(0, SIDE * SIDE * NBD // 2, one, 0)


def place(source, here, first, second):
    smem = pl.BlockSpec(memory_space=pltpu.SMEM)
    vmem = pl.BlockSpec(memory_space=pltpu.VMEM)
    return pl.pallas_call(
        place_kernel,
        in_specs=[smem, smem, vmem, vmem],
        out_specs=vmem,
        out_shape=jax.ShapeDtypeStruct((PIECE, SIDE * SIDE * NBD * BS), jnp.bfloat16),
        compiler_params=pltpu.CompilerParams(vmem_limit_bytes=24 * MIB),
    )(source, here, first, second)


def per_device(three_centre, tensor_pattern, coefficients, readers):
    groups = SIDE * SIDE
    me = lax.axis_index("atom")
    lane = lax.axis_index("fit")
    mine = coefficients.reshape(NOCC, NBD, 32, 2).transpose(1, 3, 0, 2).reshape(NBD, 2 * NOCC, 32)
    everyone = lax.all_to_all(
        jnp.broadcast_to(mine[None], (groups,) + mine.shape), "atom", 0, 0, tiled=True
    ).reshape(groups * NBD, 2 * NOCC, 32)
    picked = jnp.take(everyone, tensor_pattern.reshape(-1), axis=0)
    picked = picked.reshape(NBD, KB, 2 * NOCC, 32).transpose(0, 2, 1, 3).reshape(NBD, 2 * NOCC, 128)
    own = fit_rows(three_centre, picked)

    by_group = readers.reshape(groups, NBD, 4)
    pairs = jnp.asarray(PAIRS)[me]
    hit = jnp.any(by_group[pairs[:, 0]] == pairs[:, 1][:, None, None], axis=2)
    numbers = jnp.arange(NBD, dtype=jnp.int32)
    earlier = numbers[:, None] < numbers[None, :]
    rank = jnp.sum((hit[:, :, None] & earlier[None]).astype(jnp.int32), axis=1)
    slots = jnp.arange(CAP, dtype=jnp.int32)
    chosen = hit[:, None, :] & (rank[:, None, :] == slots[None, :, None])
    lists = jnp.sum(chosen.astype(jnp.int32) * numbers[None, None, :], axis=2)
    reads = jnp.any(by_group == me, axis=2)
    read_rank = jnp.sum((reads[:, :, None] & earlier[None]).astype(jnp.int32), axis=1)
    source = jnp.where(reads, 2 * jnp.asarray(BASE_OF)[me][:, None] + read_rank, -1)
    source = jnp.where(jnp.arange(groups)[:, None] == me, numbers[None, :], source).reshape(-1)

    held = {(0, (0, 0)): (own[0], None), (1, (0, 0)): (own[1], None)}
    for turn in range(1, 6):
        arrived = {}
        for way, step in STEP.items():
            jobs = [p for p in PLAN if p[0] == turn and p[4] == way]
            if not jobs:
                continue
            if jobs[0][5]:
                payload = held[jobs[0][1], jobs[0][3]][0]
            else:
                rows = [lists[len(OFFSETS) + LEAVES.index(p)] for p in jobs]
                payload = pack(
                    held[jobs[0][1], jobs[0][3]][0],
                    held[jobs[1][1], jobs[1][3]][0],
                    jnp.concatenate(rows),
                )
            route = [(number(a), number(plus(a, step))) for a in PLACES]
            landed = lax.ppermute(payload, "atom", route)
            for position, p in enumerate(jobs):
                arrived[p[1], p[2]] = (landed, None if p[5] else position)
        held.update(arrived)

    scale = 1.0 / math.sqrt(FIT * 2 * HALF)
    shares = []
    for number_of, chunk in enumerate(CHUNKS):
        buffer = None
        first_tile = 0 if number_of == 0 else COUNT[0]
        jobs = []
        if number_of == 0:
            for part in range(2):
                index = np.tile(np.arange(part * CAP, (part + 1) * CAP, dtype=np.int32), 2)
                jobs.append((own, jnp.asarray(index), part * TILES))
        for o in chunk:
            far = [held[half, o] for half in range(2)]
            row = lists[OFFSETS.index(o)]
            index = [row if at is None else slots + at * CAP for _, at in far]
            jobs.append(((far[0][0], far[1][0]), jnp.concatenate(index), BASE[o] - first_tile))
        for far, index, tile in jobs:
            buffer = product(own, far, index, buffer, tile, COUNT[number_of], scale)
        shares.append(lax.psum_scatter(buffer, "fit", scatter_dimension=0, tiled=True))
    return place(source, jnp.stack([me, lane]).astype(jnp.int32), shares[0], shares[1])


def solution(mesh):
    placed = (P("atom", None, "fit", None), P("atom", None), P(None, "atom"), P())
    return jax.shard_map(
        per_device, mesh=mesh, in_specs=placed, out_specs=P(("atom", "fit"), None), check_vma=False
    )
```

```python
import functools
import math

import jax
import jax.numpy as jnp
import numpy as np
from jax import lax
from jax.experimental import pallas as pl
from jax.experimental.pallas import tpu as pltpu
from jax.sharding import PartitionSpec as P

BS = 64
KB = 4
NBD = 12
CAP = 6
NP = 48
GAP = 56
NOCC = 32
HALF = NP * NOCC // 2
SIDE = 4
FIT = 8
ROWS = NBD * BS
PIECE = ROWS // FIT
MIB = 2**20

STEP = {"+y": (1, 0), "-y": (3, 0), "+z": (0, 1), "-z": (0, 3)}
NEAR = tuple(STEP.values())
MIDDLE = ((2, 0), (0, 2))
FAR = (((2, 2), (2, 0)), ((2, 2), (0, 2)))
CORNERS = (((1, 3), (0, 3)), ((3, 1), (0, 1)), ((1, 1), (1, 0)), ((3, 3), (3, 0)))
EDGES = (((2, 1), (2, 0)), ((2, 3), (2, 0)), ((1, 2), (0, 2)), ((3, 2), (0, 2)))
LEAVES = CORNERS + EDGES + FAR
CHUNKS = (
    NEAR,
    MIDDLE + tuple(o for o, _ in CORNERS),
    tuple(o for o, _ in EDGES) + ((2, 2),),
)
TILES = CAP // 2
OWN_TILES = NBD // 2
BASE = {(0, 0): 0}
for _o in sum(CHUNKS, ()):
    BASE[_o] = OWN_TILES + TILES * (len(BASE) - 1)
COUNT = tuple(TILES * len(c) + (OWN_TILES if n == 0 else 0) for n, c in enumerate(CHUNKS))
TOTAL = sum(COUNT)


def minus(a, b):
    return ((a[0] - b[0]) % SIDE, (a[1] - b[1]) % SIDE)


def plus(a, b):
    return ((a[0] + b[0]) % SIDE, (a[1] + b[1]) % SIDE)


def number(a):
    return a[0] * SIDE + a[1]


PLACES = tuple((y, z) for y in range(SIDE) for z in range(SIDE))
WHOLE = NEAR + MIDDLE
PAIRS = np.array(
    [
        [(number(minus(me, o)), number(me)) for o in WHOLE]
        + [
            (number(minus(me, sender)), number(plus(me, minus(o, sender))))
            for o, sender in LEAVES
        ]
        for me in PLACES
    ],
    dtype=np.int32,
)
BASE_OF = np.array([[BASE[minus(me, h)] for h in PLACES] for me in PLACES], dtype=np.int32)


def fit_kernel(tile_ref, coeff_ref, out_ref, lines):
    for m in range(2):
        for k in range(KB):
            for pair in range(BS // 2):
                value = tile_ref[m, k, :, pair * 128 : (pair + 1) * 128]
                lines[m, pl.ds((k * 32 + pair) * GAP, NP), :] = value.astype(jnp.float32)
    for group in range(NP // 4):
        both = []
        for m in range(2):
            parts = []
            for p in range(group * 4, group * 4 + 4):
                rows = lines[m, pl.ds(p, 128, stride=GAP), :].astype(jnp.bfloat16)
                product = jnp.dot(coeff_ref[m], rows, preferred_element_type=jnp.float32)
                parts.append(product[0:NOCC] + pltpu.roll(product[NOCC:], 64, 1))
            both.append(jnp.concatenate(parts, axis=0)[:, 0:BS])
        turned = jnp.concatenate(both, axis=1).T.astype(jnp.bfloat16)
        place = (group % 6) * 128
        out_ref[group // 6, 0, :, place : place + 128] = turned[0:BS]
        out_ref[group // 6, 1, :, place : place + 128] = turned[BS:]


def fit_rows(three_centre, picked):
    return pl.pallas_call(
        fit_kernel,
        grid=(NBD // 2,),
        in_specs=[
            pl.BlockSpec((2, KB, NP, BS * BS), lambda g: (g, 0, 0, 0)),
            pl.BlockSpec((2, 2 * NOCC, 128), lambda g: (g, 0, 0)),
        ],
        out_specs=pl.BlockSpec((2, 2, BS, HALF), lambda g: (0, g, 0, 0)),
        out_shape=jax.ShapeDtypeStruct((2, NBD, BS, HALF), jnp.bfloat16),
        scratch_shapes=[pltpu.VMEM((2, KB * 32 * GAP, 128), jnp.float32)],
        compiler_params=pltpu.CompilerParams(vmem_limit_bytes=58 * MIB),
    )(three_centre, picked)


def pack_kernel(jobs, n_in, index_ref, *refs):
    ins, outs, sems = refs[:n_in], refs[n_in:-1], refs[-1]
    copies = []
    for out, parts in zip(outs, jobs, strict=True):
        at = 0
        for source, row, first in parts:
            if row is None:
                copies.append((ins[source].at[pl.ds(first, NBD)], out.at[pl.ds(at, NBD)]))
                at += NBD
                continue
            for s in range(CAP):
                copies.append((ins[source].at[first + index_ref[row, s]], out.at[at + s]))
            at += CAP
    copies = [pltpu.make_async_copy(*copy, sems.at[n]) for n, copy in enumerate(copies)]
    for copy in copies:
        copy.start()
    for copy in copies:
        copy.wait()


def pack(jobs, sources, index, after):
    count = [sum(NBD if row is None else CAP for _, row, _ in parts) for parts in jobs]
    copies = sum(1 if row is None else CAP for parts in jobs for _, row, _ in parts)
    operands = [*sources, *after]
    return pl.pallas_call(
        functools.partial(pack_kernel, jobs, len(operands)),
        in_specs=[pl.BlockSpec(memory_space=pltpu.SMEM)]
        + [pl.BlockSpec(memory_space=pl.ANY)] * len(operands),
        out_specs=[pl.BlockSpec(memory_space=pltpu.VMEM)] * len(jobs),
        out_shape=[jax.ShapeDtypeStruct((n, BS, HALF), jnp.bfloat16) for n in count],
        scratch_shapes=[pltpu.SemaphoreType.DMA((copies,))],
        compiler_params=pltpu.CompilerParams(vmem_limit_bytes=58 * MIB),
        cost_estimate=pl.CostEstimate(flops=0, bytes_accessed=MIB, transcendentals=0),
    )(index, *operands)


def product_kernel(scale, jobs, n_in, split, index_ref, here_ref, own_ref, *refs):
    ins, outs = refs[:n_in], refs[n_in:-4]
    left, side, own_sems, sems = refs[-4:]
    step = pl.program_id(0)
    core = here_ref[1] & 1

    def own_copies():
        made = []
        for half in range(2):
            for n in range(FIT):
                piece = n
                if split:
                    piece = 2 * (n % (FIT // 2)) + (core if n < FIT // 2 else 1 - core)
                given = own_ref.at[half, pl.ds(pl.multiple_of(piece * PIECE, 32), PIECE)]
                made.append((given, left.at[half, pl.ds(n * PIECE, PIECE)], own_sems.at[half, n]))
        return [pltpu.make_async_copy(*copy) for copy in made]

    def copies(job, slot):
        made = []
        for half, (source, row, first) in enumerate(jobs[job]):
            if row is None:
                given = ins[source].at[pl.ds(first, CAP)]
                made.append((given, side.at[slot, half], sems.at[slot, half, 0]))
                continue
            for s in range(CAP):
                given = ins[source].at[first + index_ref[row, s]]
                made.append((given, side.at[slot, half, s], sems.at[slot, half, s]))
        return [pltpu.make_async_copy(*copy) for copy in made]

    def begin(job):
        for copy in copies(job, job % 2):
            copy.start()

    @pl.when(step == 0)
    def _():
        for copy in own_copies():
            copy.start()
        begin(0)
        for copy in own_copies():
            copy.wait()

    for job in range(len(jobs)):

        @pl.when(step == job)
        def _(job=job):
            if job + 1 < len(jobs):
                begin(job + 1)
            for copy in copies(job, job % 2):
                copy.wait()

    slot = lax.rem(step, 2)
    last = (((1,), (1,)), ((), ()))
    side_a = side[slot, 0].reshape(CAP * BS, HALF)
    side_b = side[slot, 1].reshape(CAP * BS, HALF)
    total = lax.dot_general(left[0], side_a, last, preferred_element_type=jnp.float32)
    total += lax.dot_general(left[1], side_b, last, preferred_element_type=jnp.float32)
    total = (total * scale).astype(jnp.bfloat16)
    pieces = FIT // len(outs)
    for n in range(FIT):
        for t in range(TILES):
            part = total[n * PIECE : (n + 1) * PIECE, t * 128 : (t + 1) * 128]
            outs[n // pieces][n % pieces, t] = part


def product(
    own, jobs, sources, index, here, buffers, tile, count, scale, after, split, cost
):
    anywhere = pl.BlockSpec(memory_space=pl.ANY)
    smem = pl.BlockSpec(memory_space=pltpu.SMEM)
    extra = list(after) + list(buffers)
    given = [own.reshape(2, ROWS, HALF), *sources, *extra]
    operands = [index, here, *given]
    pieces = FIT // 2 if split else FIT
    shape = (pieces, count, PIECE, 128)
    kinds = [jnp.bfloat16] * (2 if split else 1)
    out = pl.BlockSpec((pieces, TILES, PIECE, 128), lambda j: (0, tile // TILES + j, 0, 0))
    return pl.pallas_call(
        functools.partial(product_kernel, scale, jobs, len(sources) + len(extra), split),
        grid=(len(jobs),),
        in_specs=[smem, smem] + [anywhere] * len(given),
        out_specs=[out] * len(kinds),
        out_shape=[jax.ShapeDtypeStruct(shape, kind) for kind in kinds],
        scratch_shapes=[
            pltpu.VMEM((2, ROWS, HALF), jnp.bfloat16),
            pltpu.VMEM((2, 2, CAP, BS, HALF), jnp.bfloat16),
            pltpu.SemaphoreType.DMA((2, FIT)),
            pltpu.SemaphoreType.DMA((2, 2, CAP)),
        ],
        input_output_aliases={len(operands) - len(buffers) + n: n for n in range(len(buffers))},
        compiler_params=pltpu.CompilerParams(vmem_limit_bytes=58 * MIB),
        cost_estimate=pl.CostEstimate(flops=cost, bytes_accessed=MIB, transcendentals=0),
    )(*operands)


def add_kernel(here_ref, keep_ref, came_ref, own_ref, *send_refs):
    x = here_ref[1] >> 1
    own_ref[...] = keep_ref[x].astype(jnp.float32) + came_ref[x].astype(jnp.float32)
    for shift, send_ref in zip((1, 2, 3), send_refs, strict=True):
        there = (x + shift) & (SIDE - 1)
        value = keep_ref[there].astype(jnp.float32) + came_ref[there].astype(jnp.float32)
        send_ref[...] = value.astype(jnp.bfloat16)


def add_all_kernel(keep_ref, came_ref, out_ref):
    total = keep_ref[...].astype(jnp.float32) + came_ref[...].astype(jnp.float32)
    out_ref[...] = total.astype(jnp.bfloat16)


def add_cores_all(keep, came):
    block = pl.BlockSpec((FIT // 2, TILES, PIECE, 128), lambda j: (0, j, 0, 0))
    return pl.pallas_call(
        add_all_kernel,
        grid=(keep.shape[1] // TILES,),
        in_specs=[block, block],
        out_specs=block,
        out_shape=jax.ShapeDtypeStruct(keep.shape, jnp.bfloat16),
        compiler_params=pltpu.CompilerParams(vmem_limit_bytes=58 * MIB),
        cost_estimate=pl.CostEstimate(flops=0, bytes_accessed=MIB, transcendentals=0),
    )(keep, came)


def add_cores(here, keep, came):
    count = keep.shape[1]
    block = pl.BlockSpec((FIT // 2, TILES, PIECE, 128), lambda j: (0, j, 0, 0))
    out = pl.BlockSpec((TILES, PIECE, 128), lambda j: (j, 0, 0))
    shape = (count, PIECE, 128)
    return pl.pallas_call(
        add_kernel,
        grid=(count // TILES,),
        in_specs=[pl.BlockSpec(memory_space=pltpu.SMEM), block, block],
        out_specs=[out] * 4,
        out_shape=[jax.ShapeDtypeStruct(shape, jnp.float32)]
        + [jax.ShapeDtypeStruct(shape, jnp.bfloat16)] * 3,
        compiler_params=pltpu.CompilerParams(vmem_limit_bytes=58 * MIB),
        cost_estimate=pl.CostEstimate(flops=0, bytes_accessed=MIB, transcendentals=0),
    )(here, keep, came)


def sum_kernel(given_ref, out_ref):
    value = given_ref[0].astype(jnp.float32)
    for n in range(1, given_ref.shape[0]):
        value += given_ref[n].astype(jnp.float32)
    out_ref[0] = value.astype(jnp.bfloat16)
    for t in range(TILES):
        out_ref[1, t] = pltpu.roll(value[t], 64, 1).astype(jnp.bfloat16)


def sum_pieces(given):
    count = given.shape[1]
    return pl.pallas_call(
        sum_kernel,
        grid=(count // TILES,),
        in_specs=[pl.BlockSpec((given.shape[0], TILES, PIECE, 128), lambda j: (0, j, 0, 0))],
        out_specs=pl.BlockSpec((2, TILES, PIECE, 128), lambda j: (0, j, 0, 0)),
        out_shape=jax.ShapeDtypeStruct((2, count, PIECE, 128), jnp.bfloat16),
        compiler_params=pltpu.CompilerParams(vmem_limit_bytes=58 * MIB),
        cost_estimate=pl.CostEstimate(flops=0, bytes_accessed=MIB, transcendentals=0),
    )(given)


def place_kernel(left_ref, right_ref, here_ref, *refs):
    parts, (out_ref, own, came, tiles, sems) = refs[:-5], refs[-5:]
    copies = []
    begin = 0
    for n, count in enumerate(COUNT[:2]):
        for turned in range(2):
            to = tiles.at[pl.ds(turned * (TOTAL + 1) + begin, count)]
            copies.append((parts[n].at[turned], to, sems.at[len(copies)]))
        begin += count
    copies.append((parts[2], own, sems.at[4]))
    copies += [(parts[3 + m], came.at[m], sems.at[5 + m]) for m in range(3)]
    copies = [pltpu.make_async_copy(*copy) for copy in copies]
    for copy in copies:
        copy.start()
    tiles[TOTAL] = jnp.zeros((PIECE, 128), jnp.bfloat16)
    for copy in copies:
        copy.wait()

    def add(tile, _):
        value = own[tile]
        for m in range(3):
            value += came[m, tile].astype(jnp.float32)
        tiles[begin + tile] = value.astype(jnp.bfloat16)
        tiles[TOTAL + 1 + begin + tile] = pltpu.roll(value, 64, 1).astype(jnp.bfloat16)
        return 0

    lax.fori_loop(0, COUNT[2], add, 0, unroll=3)
    is_left = lax.broadcasted_iota(jnp.int32, (PIECE, 128), 1) < 64

    def one(pair, _):
        value = jnp.where(is_left, tiles[left_ref[pair]], tiles[right_ref[pair]])
        out_ref[:, pl.ds(pl.multiple_of(pair * 128, 128), 128)] = value
        return 0

    lax.fori_loop(0, SIDE * SIDE * NBD // 2, one, 0, unroll=4)
    lane = lax.broadcasted_iota(jnp.int32, (PIECE, 128), 1)
    line = lax.broadcasted_iota(jnp.int32, (PIECE, 128), 0)
    row_block = (line + here_ref[1] * PIECE) >> 6
    for pair in range(NBD // 2):
        at = pl.ds(pl.multiple_of((here_ref[0] * (NBD // 2) + pair) * 128, 128), 128)
        value = out_ref[:, at].astype(jnp.float32)
        value = jnp.where(row_block == 2 * pair + (lane >> 6), 0.0, value)
        out_ref[:, at] = value.astype(jnp.bfloat16)


def place(source, here, parts):
    tile, odd = source >> 1, source & 1
    left = jnp.where(source < 0, TOTAL, jnp.where(odd == 0, tile, tile + TOTAL + 1))[0::2]
    right = jnp.where(source < 0, TOTAL, jnp.where(odd == 1, tile, tile + TOTAL + 1))[1::2]
    smem = pl.BlockSpec(memory_space=pltpu.SMEM)
    return pl.pallas_call(
        place_kernel,
        in_specs=[smem, smem, smem] + [pl.BlockSpec(memory_space=pl.ANY)] * len(parts),
        out_specs=pl.BlockSpec(memory_space=pltpu.VMEM),
        out_shape=jax.ShapeDtypeStruct((PIECE, SIDE * SIDE * NBD * BS), jnp.bfloat16),
        scratch_shapes=[
            pltpu.VMEM((COUNT[2], PIECE, 128), jnp.float32),
            pltpu.VMEM((3, COUNT[2], PIECE, 128), jnp.bfloat16),
            pltpu.VMEM((2 * TOTAL + 1, PIECE, 128), jnp.bfloat16),
            pltpu.SemaphoreType.DMA((8,)),
        ],
        compiler_params=pltpu.CompilerParams(vmem_limit_bytes=58 * MIB),
    )(left, right, here, *parts)


def per_device(three_centre, tensor_pattern, coefficients, readers):
    groups = SIDE * SIDE
    me = lax.axis_index("atom")
    lane = lax.axis_index("fit")
    mine = coefficients.reshape(NOCC, NBD, 32, 2).transpose(1, 3, 0, 2).reshape(NBD, 2 * NOCC, 32)
    everyone = lax.all_to_all(
        jnp.broadcast_to(mine[None], (groups,) + mine.shape), "atom", 0, 0, tiled=True
    ).reshape(groups * NBD, 2 * NOCC, 32)
    picked = jnp.take(everyone, tensor_pattern.reshape(-1), axis=0)
    picked = picked.reshape(NBD, KB, 2 * NOCC, 32).transpose(0, 2, 1, 3).reshape(NBD, 2 * NOCC, 128)
    own = fit_rows(three_centre, picked)

    by_group = readers.reshape(groups, NBD, 4)
    pairs = jnp.asarray(PAIRS)[me]
    hit = jnp.any(by_group[pairs[:, 0]] == pairs[:, 1][:, None, None], axis=2)
    numbers = jnp.arange(NBD, dtype=jnp.int32)
    earlier = numbers[:, None] < numbers[None, :]
    rank = jnp.sum((hit[:, :, None] & earlier[None]).astype(jnp.int32), axis=1)
    slots = jnp.arange(CAP, dtype=jnp.int32)
    chosen = hit[:, None, :] & (rank[:, None, :] == slots[None, :, None])
    lists = jnp.sum(chosen.astype(jnp.int32) * numbers[None, None, :], axis=2)
    reads = jnp.any(by_group == me, axis=2)
    read_rank = jnp.sum((reads[:, :, None] & earlier[None]).astype(jnp.int32), axis=1)
    source = jnp.where(reads, 2 * jnp.asarray(BASE_OF)[me][:, None] + read_rank, -1)
    source = jnp.where(jnp.arange(groups)[:, None] == me, numbers[None, :], source).reshape(-1)

    scale = 1.0 / math.sqrt(FIT * 2 * HALF)
    def send(payload, step):
        route = [(number(a), number(plus(a, step))) for a in PLACES]
        return lax.ppermute(payload, "atom", route)

    here = jnp.stack([me, lane]).astype(jnp.int32)

    def multiply(jobs, buffers, tile, count, after, split=False, cost=0):
        sources = []
        for pair in jobs:
            for array, _, _ in pair:
                if not any(array is known for known in sources):
                    sources.append(array)
        at = lambda array: next(n for n, known in enumerate(sources) if known is array)
        jobs = tuple(tuple((at(array), row, first) for array, row, first in p) for p in jobs)
        return product(
            own, jobs, sources, lists, here, buffers, tile, count, scale, after, split, cost
        )

    def over_cores(to_send):
        return lax.ppermute(to_send, "fit", [(n, n ^ 1) for n in range(FIT)])

    def over_chips(pieces):
        sent = []
        for shift, piece in zip((1, 2, 3), pieces, strict=True):
            route = [(n, (n + 2 * shift) % FIT) for n in range(FIT)]
            sent.append(lax.ppermute(piece, "fit", route))
        return sent

    def exchange(pieces):
        groups = [list(range(core, FIT, 2)) for core in range(2)]
        return lax.all_to_all(pieces, "fit", 0, 0, axis_index_groups=groups, tiled=True)

    def leaf_row(o):
        return len(WHOLE) + [p[0] for p in LEAVES].index(o)

    def both(source, row):
        return ((source, row, 0), (source, row, NBD))

    def hop(leaf):
        return minus(*leaf)

    own = own.reshape(2 * NBD, BS, HALF)
    near = [send(own, o) for o in NEAR]
    jobs = [[(own, None, half * NBD + part * CAP) for half in range(2)] for part in range(2)]
    partial = multiply(jobs, [], 0, COUNT[0], [], True)
    jobs = []
    for n, (o, sender) in enumerate(CORNERS):
        jobs.append(((n, None, (n % 2) * NBD), *both(NEAR.index(sender), leaf_row(o))))
    packed = pack(tuple(jobs), near, lists, partial[:1])
    second = [send(packed[n], o) for n, o in enumerate(NEAR)]
    jobs = [[(near[n], n, 0), (near[n], n, NBD)] for n in range(4)]
    keep, to_send = multiply(jobs, partial, OWN_TILES, COUNT[0], packed[:1], True)
    first_pieces = add_cores_all(keep, over_cores(to_send))
    jobs = []
    for o, sender in EDGES:
        m, row = 2 * MIDDLE.index(sender), leaf_row(o)
        jobs.append(((m, row, 0), (m + 1, row, 0)))
    jobs.append(((0, leaf_row((2, 2)), 0),))
    packed = pack(tuple(jobs), second, lists, [first_pieces])
    last = [send(packed[4], hop(FAR[0]))]
    third = [send(packed[n], hop(leaf)) for n, leaf in enumerate(EDGES)]
    first_came = exchange(first_pieces)
    jobs = [[(second[2 * m], 4 + m, 0), (second[2 * m + 1], 4 + m, 0)] for m in range(2)]
    jobs += [[(second[n], None, NBD), (second[n], None, NBD + CAP)] for n in range(4)]
    (partial,) = multiply(jobs, [], 0, COUNT[1], packed[:1])
    second_came = lax.all_to_all(partial, "fit", 0, 0, tiled=True)
    jobs = (((0, leaf_row((2, 2)) + 1, 0),),)
    last.append(send(pack(jobs, second[3:], lists, [partial])[0], hop(FAR[1])))
    jobs = [[(array, None, 0), (array, None, CAP)] for array in third]
    jobs.append([(array, None, 0) for array in last])
    keep, to_send = multiply(jobs, [], 0, COUNT[2], [first_came], True, 10**12)
    pieces = add_cores(here, keep, over_cores(to_send))
    third_came = over_chips(pieces[1:])
    parts = [sum_pieces(first_came), sum_pieces(second_came), pieces[0], *third_came]
    return place(source, here, parts)


def solution(mesh):
    placed = (P("atom", None, "fit", None), P("atom", None), P(None, "atom"), P())
    return jax.shard_map(
        per_device, mesh=mesh, in_specs=placed, out_specs=P(("atom", "fit"), None), check_vma=False
    )
```

```python
import functools
import math

import jax
import jax.numpy as jnp
import numpy as np
from jax import lax
from jax.experimental import pallas as pl
from jax.experimental.pallas import tpu as pltpu
from jax.sharding import PartitionSpec as P

BS = 64
KB = 4
NBD = 12
CAP = 6
NP = 48
GAP = 56
NOCC = 32
HALF = NP * NOCC // 2
SIDE = 4
FIT = 8
ROWS = NBD * BS
PIECE = ROWS // FIT
MIB = 2**20

STEP = {"+y": (1, 0), "-y": (3, 0), "+z": (0, 1), "-z": (0, 3)}
NEAR = tuple(STEP.values())
MIDDLE = ((2, 0), (0, 2))
FAR = (((2, 2), (2, 0)), ((2, 2), (0, 2)))
CORNERS = (((1, 3), (0, 3)), ((3, 1), (0, 1)), ((1, 1), (1, 0)), ((3, 3), (3, 0)))
EDGES = (((2, 1), (2, 0)), ((2, 3), (2, 0)), ((1, 2), (0, 2)), ((3, 2), (0, 2)))
LEAVES = CORNERS + EDGES + FAR
CHUNKS = (
    NEAR,
    MIDDLE + tuple(o for o, _ in CORNERS),
    tuple(o for o, _ in EDGES) + ((2, 2),),
)
TILES = CAP // 2
OWN_TILES = NBD // 2
BASE = {(0, 0): 0}
for _o in sum(CHUNKS, ()):
    BASE[_o] = OWN_TILES + TILES * (len(BASE) - 1)
COUNT = tuple(TILES * len(c) + (OWN_TILES if n == 0 else 0) for n, c in enumerate(CHUNKS))
TOTAL = sum(COUNT)


def minus(a, b):
    return ((a[0] - b[0]) % SIDE, (a[1] - b[1]) % SIDE)


def plus(a, b):
    return ((a[0] + b[0]) % SIDE, (a[1] + b[1]) % SIDE)


def number(a):
    return a[0] * SIDE + a[1]


PLACES = tuple((y, z) for y in range(SIDE) for z in range(SIDE))
WHOLE = NEAR + MIDDLE
PAIRS = np.array(
    [
        [(number(minus(me, o)), number(me)) for o in WHOLE]
        + [
            (number(minus(me, sender)), number(plus(me, minus(o, sender))))
            for o, sender in LEAVES
        ]
        for me in PLACES
    ],
    dtype=np.int32,
)
BASE_OF = np.array([[BASE[minus(me, h)] for h in PLACES] for me in PLACES], dtype=np.int32)


def spread_matrices():
    table = np.zeros((KB, 128, 256), np.float32)
    for k in range(KB):
        for l in range(BS):
            table[k, l, (l % 2) * 128 + k * 32 + l // 2] = 1.0
    return table


def fit_kernel(where_ref, tile_ref, coeff_ref, spread_ref, out_ref, lines, chosen):
    step = pl.program_id(0)

    @pl.when(step == 0)
    def _():
        for n in range(NBD):
            total = jnp.zeros((NOCC, 256), jnp.float32)
            for k in range(KB):
                lane = pl.ds(pl.multiple_of(where_ref[1, n * KB + k] * 128, 128), 128)
                tile = coeff_ref[where_ref[0, n * KB + k], :, lane].astype(jnp.float32)
                odd = where_ref[2, n * KB + k] == 1
                tile = jnp.where(odd, pltpu.roll(tile, BS, 1), tile).astype(jnp.bfloat16)
                total += jnp.dot(tile, spread_ref[k], preferred_element_type=jnp.float32)
            both = jnp.concatenate([total[:, 0:128], total[:, 128:256]], axis=0)
            chosen[n] = both.astype(jnp.bfloat16)

    for m in range(2):
        for k in range(KB):
            for pair in range(BS // 2):
                value = tile_ref[m, k, :, pair * 128 : (pair + 1) * 128]
                lines[m, pl.ds((k * 32 + pair) * GAP, NP), :] = value.astype(jnp.float32)
    for group in range(NP // 4):
        both = []
        for m in range(2):
            parts = []
            for p in range(group * 4, group * 4 + 4):
                rows = lines[m, pl.ds(p, 128, stride=GAP), :].astype(jnp.bfloat16)
                product = jnp.dot(chosen[2 * step + m], rows, preferred_element_type=jnp.float32)
                parts.append(product[0:NOCC] + pltpu.roll(product[NOCC:], 64, 1))
            both.append(jnp.concatenate(parts, axis=0)[:, 0:BS])
        turned = jnp.concatenate(both, axis=1).T.astype(jnp.bfloat16)
        place = (group % 6) * 128
        out_ref[group // 6, 0, :, place : place + 128] = turned[0:BS]
        out_ref[group // 6, 1, :, place : place + 128] = turned[BS:]


def fit_rows(three_centre, where, everyone):
    spread = jnp.asarray(spread_matrices(), jnp.bfloat16)
    return pl.pallas_call(
        fit_kernel,
        grid=(NBD // 2,),
        in_specs=[
            pl.BlockSpec(memory_space=pltpu.SMEM),
            pl.BlockSpec((2, KB, NP, BS * BS), lambda g: (g, 0, 0, 0)),
            pl.BlockSpec(everyone.shape, lambda g: (0, 0, 0)),
            pl.BlockSpec(spread.shape, lambda g: (0, 0, 0)),
        ],
        out_specs=pl.BlockSpec((2, 2, BS, HALF), lambda g: (0, g, 0, 0)),
        out_shape=jax.ShapeDtypeStruct((2, NBD, BS, HALF), jnp.bfloat16),
        scratch_shapes=[
            pltpu.VMEM((2, KB * 32 * GAP, 128), jnp.float32),
            pltpu.VMEM((NBD, 2 * NOCC, 128), jnp.bfloat16),
        ],
        compiler_params=pltpu.CompilerParams(vmem_limit_bytes=58 * MIB),
        cost_estimate=pl.CostEstimate(flops=2**30, bytes_accessed=20 * MIB, transcendentals=0),
    )(where, three_centre, everyone, spread)


def pack_kernel(jobs, n_in, index_ref, *refs):
    ins, outs, sems = refs[:n_in], refs[n_in:-1], refs[-1]
    copies = []
    for out, parts in zip(outs, jobs, strict=True):
        at = 0
        for source, row, first in parts:
            if row is None:
                copies.append((ins[source].at[pl.ds(first, NBD)], out.at[pl.ds(at, NBD)]))
                at += NBD
                continue
            for s in range(CAP):
                copies.append((ins[source].at[first + index_ref[row, s]], out.at[at + s]))
            at += CAP
    copies = [pltpu.make_async_copy(*copy, sems.at[n]) for n, copy in enumerate(copies)]
    for copy in copies:
        copy.start()
    for copy in copies:
        copy.wait()


def pack(jobs, sources, index, after):
    count = [sum(NBD if row is None else CAP for _, row, _ in parts) for parts in jobs]
    copies = sum(1 if row is None else CAP for parts in jobs for _, row, _ in parts)
    operands = [*sources, *after]
    return pl.pallas_call(
        functools.partial(pack_kernel, jobs, len(operands)),
        in_specs=[pl.BlockSpec(memory_space=pltpu.SMEM)]
        + [pl.BlockSpec(memory_space=pl.ANY)] * len(operands),
        out_specs=[pl.BlockSpec(memory_space=pltpu.VMEM)] * len(jobs),
        out_shape=[jax.ShapeDtypeStruct((n, BS, HALF), jnp.bfloat16) for n in count],
        scratch_shapes=[pltpu.SemaphoreType.DMA((copies,))],
        compiler_params=pltpu.CompilerParams(vmem_limit_bytes=58 * MIB),
        cost_estimate=pl.CostEstimate(flops=0, bytes_accessed=MIB, transcendentals=0),
    )(index, *operands)


def product_kernel(scale, jobs, n_in, split, index_ref, here_ref, own_ref, *refs):
    ins, outs = refs[:n_in], refs[n_in:-4]
    left, side, own_sems, sems = refs[-4:]
    step = pl.program_id(0)
    core = here_ref[1] & 1

    def own_copies():
        made = []
        for half in range(2):
            for n in range(FIT):
                piece = n
                if split:
                    piece = 2 * (n % (FIT // 2)) + (core if n < FIT // 2 else 1 - core)
                given = own_ref.at[half, pl.ds(pl.multiple_of(piece * PIECE, 32), PIECE)]
                made.append((given, left.at[half, pl.ds(n * PIECE, PIECE)], own_sems.at[half, n]))
        return [pltpu.make_async_copy(*copy) for copy in made]

    def copies(job, slot):
        made = []
        for half, (source, row, first) in enumerate(jobs[job]):
            if row is None:
                given = ins[source].at[pl.ds(first, CAP)]
                made.append((given, side.at[slot, half], sems.at[slot, half, 0]))
                continue
            for s in range(CAP):
                given = ins[source].at[first + index_ref[row, s]]
                made.append((given, side.at[slot, half, s], sems.at[slot, half, s]))
        return [pltpu.make_async_copy(*copy) for copy in made]

    def begin(job):
        for copy in copies(job, job % 2):
            copy.start()

    @pl.when(step == 0)
    def _():
        for copy in own_copies():
            copy.start()
        begin(0)
        for copy in own_copies():
            copy.wait()

    for job in range(len(jobs)):

        @pl.when(step == job)
        def _(job=job):
            if job + 1 < len(jobs):
                begin(job + 1)
            for copy in copies(job, job % 2):
                copy.wait()

    slot = lax.rem(step, 2)
    last = (((1,), (1,)), ((), ()))
    side_a = side[slot, 0].reshape(CAP * BS, HALF)
    side_b = side[slot, 1].reshape(CAP * BS, HALF)
    total = lax.dot_general(left[0], side_a, last, preferred_element_type=jnp.float32)
    total += lax.dot_general(left[1], side_b, last, preferred_element_type=jnp.float32)
    total = (total * scale).astype(jnp.bfloat16)
    pieces = FIT // len(outs)
    for n in range(FIT):
        for t in range(TILES):
            part = total[n * PIECE : (n + 1) * PIECE, t * 128 : (t + 1) * 128]
            outs[n // pieces][n % pieces, t] = part


def product(
    own, jobs, sources, index, here, buffers, tile, count, scale, after, split, cost
):
    anywhere = pl.BlockSpec(memory_space=pl.ANY)
    smem = pl.BlockSpec(memory_space=pltpu.SMEM)
    extra = list(after) + list(buffers)
    given = [own.reshape(2, ROWS, HALF), *sources, *extra]
    operands = [index, here, *given]
    pieces = FIT // 2 if split else FIT
    shape = (pieces, count, PIECE, 128)
    kinds = [jnp.bfloat16] * (2 if split else 1)
    out = pl.BlockSpec((pieces, TILES, PIECE, 128), lambda j: (0, tile // TILES + j, 0, 0))
    return pl.pallas_call(
        functools.partial(product_kernel, scale, jobs, len(sources) + len(extra), split),
        grid=(len(jobs),),
        in_specs=[smem, smem] + [anywhere] * len(given),
        out_specs=[out] * len(kinds),
        out_shape=[jax.ShapeDtypeStruct(shape, kind) for kind in kinds],
        scratch_shapes=[
            pltpu.VMEM((2, ROWS, HALF), jnp.bfloat16),
            pltpu.VMEM((2, 2, CAP, BS, HALF), jnp.bfloat16),
            pltpu.SemaphoreType.DMA((2, FIT)),
            pltpu.SemaphoreType.DMA((2, 2, CAP)),
        ],
        input_output_aliases={len(operands) - len(buffers) + n: n for n in range(len(buffers))},
        compiler_params=pltpu.CompilerParams(vmem_limit_bytes=58 * MIB),
        cost_estimate=pl.CostEstimate(flops=cost, bytes_accessed=MIB, transcendentals=0),
    )(*operands)


def add_kernel(here_ref, keep_ref, came_ref, own_ref, *send_refs):
    x = here_ref[1] >> 1
    own_ref[...] = keep_ref[x].astype(jnp.float32) + came_ref[x].astype(jnp.float32)
    for shift, send_ref in zip((2, 1, 3), send_refs, strict=True):
        there = (x + shift) & (SIDE - 1)
        value = keep_ref[there].astype(jnp.float32) + came_ref[there].astype(jnp.float32)
        send_ref[...] = value.astype(jnp.bfloat16)


def add_all_kernel(keep_ref, came_ref, out_ref):
    total = keep_ref[...].astype(jnp.float32) + came_ref[...].astype(jnp.float32)
    out_ref[...] = total.astype(jnp.bfloat16)


def add_cores_all(keep, came):
    block = pl.BlockSpec((FIT // 2, TILES, PIECE, 128), lambda j: (0, j, 0, 0))
    return pl.pallas_call(
        add_all_kernel,
        grid=(keep.shape[1] // TILES,),
        in_specs=[block, block],
        out_specs=block,
        out_shape=jax.ShapeDtypeStruct(keep.shape, jnp.bfloat16),
        compiler_params=pltpu.CompilerParams(vmem_limit_bytes=58 * MIB),
        cost_estimate=pl.CostEstimate(flops=0, bytes_accessed=MIB, transcendentals=0),
    )(keep, came)


def add_cores(here, keep, came):
    count = keep.shape[1]
    step = 5 if count % 5 == 0 else TILES
    block = pl.BlockSpec((FIT // 2, step, PIECE, 128), lambda j: (0, j, 0, 0))
    out = pl.BlockSpec((step, PIECE, 128), lambda j: (j, 0, 0))
    shape = (count, PIECE, 128)
    return pl.pallas_call(
        add_kernel,
        grid=(count // step,),
        in_specs=[pl.BlockSpec(memory_space=pltpu.SMEM), block, block],
        out_specs=[out] * 4,
        out_shape=[jax.ShapeDtypeStruct(shape, jnp.float32)]
        + [jax.ShapeDtypeStruct(shape, jnp.bfloat16)] * 3,
        compiler_params=pltpu.CompilerParams(vmem_limit_bytes=58 * MIB),
        cost_estimate=pl.CostEstimate(flops=0, bytes_accessed=MIB, transcendentals=0),
    )(here, keep, came)


def sum_kernel(given_ref, out_ref):
    value = given_ref[0].astype(jnp.float32)
    for n in range(1, given_ref.shape[0]):
        value += given_ref[n].astype(jnp.float32)
    out_ref[0] = value.astype(jnp.bfloat16)
    for t in range(TILES):
        out_ref[1, t] = pltpu.roll(value[t], 64, 1).astype(jnp.bfloat16)


def sum_pieces(given):
    count = given.shape[1]
    return pl.pallas_call(
        sum_kernel,
        grid=(count // TILES,),
        in_specs=[pl.BlockSpec((given.shape[0], TILES, PIECE, 128), lambda j: (0, j, 0, 0))],
        out_specs=pl.BlockSpec((2, TILES, PIECE, 128), lambda j: (0, j, 0, 0)),
        out_shape=jax.ShapeDtypeStruct((2, count, PIECE, 128), jnp.bfloat16),
        compiler_params=pltpu.CompilerParams(vmem_limit_bytes=58 * MIB),
        cost_estimate=pl.CostEstimate(flops=0, bytes_accessed=MIB, transcendentals=0),
    )(given)


def place_kernel(left_ref, right_ref, here_ref, *refs):
    parts, (out_ref, own, came, tiles, sems) = refs[:-5], refs[-5:]
    copies = []
    begin = 0
    for n, count in enumerate(COUNT[:2]):
        for turned in range(2):
            to = tiles.at[pl.ds(turned * (TOTAL + 1) + begin, count)]
            copies.append((parts[n].at[turned], to, sems.at[len(copies)]))
        begin += count
    copies.append((parts[2], own, sems.at[4]))
    copies += [(parts[3 + m], came.at[m], sems.at[5 + m]) for m in range(3)]
    copies = [pltpu.make_async_copy(*copy) for copy in copies]
    for copy in copies:
        copy.start()
    tiles[TOTAL] = jnp.zeros((PIECE, 128), jnp.bfloat16)
    for copy in copies:
        copy.wait()

    def add(tile, _):
        value = own[tile]
        for m in range(3):
            value += came[m, tile].astype(jnp.float32)
        tiles[begin + tile] = value.astype(jnp.bfloat16)
        tiles[TOTAL + 1 + begin + tile] = pltpu.roll(value, 64, 1).astype(jnp.bfloat16)
        return 0

    lax.fori_loop(0, COUNT[2], add, 0, unroll=3)
    is_left = lax.broadcasted_iota(jnp.int32, (PIECE, 128), 1) < 64

    def one(pair, _):
        value = jnp.where(is_left, tiles[left_ref[pair]], tiles[right_ref[pair]])
        out_ref[:, pl.ds(pl.multiple_of(pair * 128, 128), 128)] = value
        return 0

    lax.fori_loop(0, SIDE * SIDE * NBD // 2, one, 0, unroll=4)
    lane = lax.broadcasted_iota(jnp.int32, (PIECE, 128), 1)
    line = lax.broadcasted_iota(jnp.int32, (PIECE, 128), 0)
    row_block = (line + here_ref[1] * PIECE) >> 6
    for pair in range(NBD // 2):
        at = pl.ds(pl.multiple_of((here_ref[0] * (NBD // 2) + pair) * 128, 128), 128)
        value = out_ref[:, at].astype(jnp.float32)
        value = jnp.where(row_block == 2 * pair + (lane >> 6), 0.0, value)
        out_ref[:, at] = value.astype(jnp.bfloat16)


def place(source, here, parts):
    tile, odd = source >> 1, source & 1
    left = jnp.where(source < 0, TOTAL, jnp.where(odd == 0, tile, tile + TOTAL + 1))[0::2]
    right = jnp.where(source < 0, TOTAL, jnp.where(odd == 1, tile, tile + TOTAL + 1))[1::2]
    smem = pl.BlockSpec(memory_space=pltpu.SMEM)
    return pl.pallas_call(
        place_kernel,
        in_specs=[smem, smem, smem] + [pl.BlockSpec(memory_space=pl.ANY)] * len(parts),
        out_specs=pl.BlockSpec(memory_space=pltpu.VMEM),
        out_shape=jax.ShapeDtypeStruct((PIECE, SIDE * SIDE * NBD * BS), jnp.bfloat16),
        scratch_shapes=[
            pltpu.VMEM((COUNT[2], PIECE, 128), jnp.float32),
            pltpu.VMEM((3, COUNT[2], PIECE, 128), jnp.bfloat16),
            pltpu.VMEM((2 * TOTAL + 1, PIECE, 128), jnp.bfloat16),
            pltpu.SemaphoreType.DMA((8,)),
        ],
        compiler_params=pltpu.CompilerParams(vmem_limit_bytes=58 * MIB),
    )(left, right, here, *parts)


def per_device(three_centre, tensor_pattern, coefficients, readers):
    groups = SIDE * SIDE
    me = lax.axis_index("atom")
    lane = lax.axis_index("fit")
    everyone = jnp.broadcast_to(coefficients[None], (groups,) + coefficients.shape)
    everyone = lax.all_to_all(everyone, "atom", 0, 0, tiled=True)
    partner = tensor_pattern.reshape(-1)
    where = jnp.stack([partner // NBD, (partner % NBD) // 2, partner % 2]).astype(jnp.int32)
    own = fit_rows(three_centre, where, everyone)

    by_group = readers.reshape(groups, NBD, 4)
    pairs = jnp.asarray(PAIRS)[me]
    hit = jnp.any(by_group[pairs[:, 0]] == pairs[:, 1][:, None, None], axis=2)
    numbers = jnp.arange(NBD, dtype=jnp.int32)
    earlier = numbers[:, None] < numbers[None, :]
    rank = jnp.sum((hit[:, :, None] & earlier[None]).astype(jnp.int32), axis=1)
    slots = jnp.arange(CAP, dtype=jnp.int32)
    chosen = hit[:, None, :] & (rank[:, None, :] == slots[None, :, None])
    lists = jnp.sum(chosen.astype(jnp.int32) * numbers[None, None, :], axis=2)
    reads = jnp.any(by_group == me, axis=2)
    read_rank = jnp.sum((reads[:, :, None] & earlier[None]).astype(jnp.int32), axis=1)
    source = jnp.where(reads, 2 * jnp.asarray(BASE_OF)[me][:, None] + read_rank, -1)
    source = jnp.where(jnp.arange(groups)[:, None] == me, numbers[None, :], source).reshape(-1)

    scale = 1.0 / math.sqrt(FIT * 2 * HALF)
    def send(payload, step):
        route = [(number(a), number(plus(a, step))) for a in PLACES]
        return lax.ppermute(payload, "atom", route)

    here = jnp.stack([me, lane]).astype(jnp.int32)

    def multiply(jobs, buffers, tile, count, after, split=False, cost=0):
        sources = []
        for pair in jobs:
            for array, _, _ in pair:
                if not any(array is known for known in sources):
                    sources.append(array)
        at = lambda array: next(n for n, known in enumerate(sources) if known is array)
        jobs = tuple(tuple((at(array), row, first) for array, row, first in p) for p in jobs)
        return product(
            own, jobs, sources, lists, here, buffers, tile, count, scale, after, split, cost
        )

    def over_cores(to_send):
        return lax.ppermute(to_send, "fit", [(n, n ^ 1) for n in range(FIT)])

    def over_chips(pieces):
        sent = []
        for shift, piece in zip((2, 1, 3), pieces, strict=True):
            route = [(n, (n + 2 * shift) % FIT) for n in range(FIT)]
            sent.append(lax.ppermute(piece, "fit", route))
        return sent

    def exchange(pieces):
        groups = [list(range(core, FIT, 2)) for core in range(2)]
        return lax.all_to_all(pieces, "fit", 0, 0, axis_index_groups=groups, tiled=True)

    def leaf_row(o):
        return len(WHOLE) + [p[0] for p in LEAVES].index(o)

    def both(source, row):
        return ((source, row, 0), (source, row, NBD))

    def hop(leaf):
        return minus(*leaf)

    own = own.reshape(2 * NBD, BS, HALF)
    near = [send(own, o) for o in NEAR]
    jobs = [[(own, None, half * NBD + part * CAP) for half in range(2)] for part in range(2)]
    partial = multiply(jobs, [], 0, COUNT[0], [], True)
    jobs = []
    for n, (o, sender) in enumerate(CORNERS):
        jobs.append(((n, None, (n % 2) * NBD), *both(NEAR.index(sender), leaf_row(o))))
    packed = pack(tuple(jobs), near, lists, partial[:1])
    second = [send(packed[n], o) for n, o in enumerate(NEAR)]
    jobs = [[(near[n], n, 0), (near[n], n, NBD)] for n in range(4)]
    keep, to_send = multiply(jobs, partial, OWN_TILES, COUNT[0], packed[:1], True)
    first_pieces = add_cores_all(keep, over_cores(to_send))
    jobs = []
    for o, sender in EDGES:
        m, row = 2 * MIDDLE.index(sender), leaf_row(o)
        jobs.append(((m, row, 0), (m + 1, row, 0)))
    jobs.append(((0, leaf_row((2, 2)), 0),))
    packed = pack(tuple(jobs), second, lists, [first_pieces])
    last = [send(packed[4], hop(FAR[0]))]
    third = [send(packed[n], hop(leaf)) for n, leaf in enumerate(EDGES)]
    first_came = exchange(first_pieces)
    jobs = [[(second[2 * m], 4 + m, 0), (second[2 * m + 1], 4 + m, 0)] for m in range(2)]
    jobs += [[(second[n], None, NBD), (second[n], None, NBD + CAP)] for n in range(4)]
    (partial,) = multiply(jobs, [], 0, COUNT[1], packed[:1])
    second_came = lax.all_to_all(partial, "fit", 0, 0, tiled=True)
    jobs = (((0, leaf_row((2, 2)) + 1, 0),),)
    last.append(send(pack(jobs, second[3:], lists, [partial])[0], hop(FAR[1])))
    jobs = [[(array, None, 0), (array, None, CAP)] for array in third]
    jobs.append([(array, None, 0) for array in last])
    keep, to_send = multiply(jobs, [], 0, COUNT[2], [first_came], True, 10**12)
    pieces = add_cores(here, keep, over_cores(to_send))
    third_came = over_chips(pieces[1:])
    parts = [sum_pieces(first_came), sum_pieces(second_came), pieces[0], *third_came]
    return place(source, here, parts)


def solution(mesh):
    placed = (P("atom", None, "fit", None), P("atom", None), P(None, "atom"), P())
    return jax.shard_map(
        per_device, mesh=mesh, in_specs=placed, out_specs=P(("atom", "fit"), None), check_vma=False
    )
```

```python
import functools
import math

import jax
import jax.numpy as jnp
import numpy as np
from jax import lax
from jax.experimental import pallas as pl
from jax.experimental.pallas import tpu as pltpu
from jax.sharding import PartitionSpec as P

BS = 64
KB = 4
NBD = 12
CAP = 6
NP = 48
GAP = 56
NOCC = 32
HALF = NP * NOCC // 2
SIDE = 4
FIT = 8
ROWS = NBD * BS
PIECE = ROWS // FIT
MIB = 2**20

STEP = {"+y": (1, 0), "-y": (3, 0), "+z": (0, 1), "-z": (0, 3)}
NEAR = tuple(STEP.values())
MIDDLE = ((2, 0), (0, 2))
FAR = (((2, 2), (2, 0)), ((2, 2), (0, 2)))
CORNERS = (((1, 3), (0, 3)), ((3, 1), (0, 1)), ((1, 1), (1, 0)), ((3, 3), (3, 0)))
EDGES = (((2, 1), (2, 0)), ((2, 3), (2, 0)), ((1, 2), (0, 2)), ((3, 2), (0, 2)))
LEAVES = CORNERS + EDGES + FAR
CHUNKS = (
    NEAR,
    MIDDLE + tuple(o for o, _ in CORNERS),
    tuple(o for o, _ in EDGES) + ((2, 2),),
)
TILES = CAP // 2
OWN_TILES = NBD // 2
BASE = {(0, 0): 0}
for _o in sum(CHUNKS, ()):
    BASE[_o] = OWN_TILES + TILES * (len(BASE) - 1)
COUNT = tuple(TILES * len(c) + (OWN_TILES if n == 0 else 0) for n, c in enumerate(CHUNKS))
TOTAL = sum(COUNT)


def minus(a, b):
    return ((a[0] - b[0]) % SIDE, (a[1] - b[1]) % SIDE)


def plus(a, b):
    return ((a[0] + b[0]) % SIDE, (a[1] + b[1]) % SIDE)


def number(a):
    return a[0] * SIDE + a[1]


PLACES = tuple((y, z) for y in range(SIDE) for z in range(SIDE))
WHOLE = NEAR + MIDDLE
PAIRS = np.array(
    [
        [(number(minus(me, o)), number(me)) for o in WHOLE]
        + [
            (number(minus(me, sender)), number(plus(me, minus(o, sender))))
            for o, sender in LEAVES
        ]
        for me in PLACES
    ],
    dtype=np.int32,
)
BASE_OF = np.array([[BASE[minus(me, h)] for h in PLACES] for me in PLACES], dtype=np.int32)


def spread_matrices():
    table = np.zeros((KB, 128, 256), np.float32)
    for k in range(KB):
        for l in range(BS):
            table[k, l, (l % 2) * 128 + k * 32 + l // 2] = 1.0
    return table


def fit_kernel(where_ref, tile_ref, coeff_ref, spread_ref, out_ref, lines, chosen):
    step = pl.program_id(0)

    @pl.when(step == 0)
    def _():
        for n in range(NBD):
            total = jnp.zeros((NOCC, 256), jnp.float32)
            for k in range(KB):
                lane = pl.ds(pl.multiple_of(where_ref[1, n * KB + k] * 128, 128), 128)
                tile = coeff_ref[where_ref[0, n * KB + k], :, lane].astype(jnp.float32)
                odd = where_ref[2, n * KB + k] == 1
                tile = jnp.where(odd, pltpu.roll(tile, BS, 1), tile).astype(jnp.bfloat16)
                total += jnp.dot(tile, spread_ref[k], preferred_element_type=jnp.float32)
            both = jnp.concatenate([total[:, 0:128], total[:, 128:256]], axis=0)
            chosen[n] = both.astype(jnp.bfloat16)

    for m in range(2):
        for k in range(KB):
            for pair in range(BS // 2):
                value = tile_ref[m, k, :, pair * 128 : (pair + 1) * 128]
                lines[m, pl.ds((k * 32 + pair) * GAP, NP), :] = value.astype(jnp.float32)
    for group in range(NP // 4):
        both = []
        for m in range(2):
            parts = []
            for p in range(group * 4, group * 4 + 4):
                rows = lines[m, pl.ds(p, 128, stride=GAP), :].astype(jnp.bfloat16)
                product = jnp.dot(chosen[2 * step + m], rows, preferred_element_type=jnp.float32)
                parts.append(product[0:NOCC] + pltpu.roll(product[NOCC:], 64, 1))
            both.append(jnp.concatenate(parts, axis=0)[:, 0:BS])
        turned = jnp.concatenate(both, axis=1).T.astype(jnp.bfloat16)
        place = (group % 6) * 128
        out_ref[group // 6, 0, :, place : place + 128] = turned[0:BS]
        out_ref[group // 6, 1, :, place : place + 128] = turned[BS:]


def fit_rows(three_centre, where, everyone):
    spread = jnp.asarray(spread_matrices(), jnp.bfloat16)
    return pl.pallas_call(
        fit_kernel,
        grid=(NBD // 2,),
        in_specs=[
            pl.BlockSpec(memory_space=pltpu.SMEM),
            pl.BlockSpec((2, KB, NP, BS * BS), lambda g: (g, 0, 0, 0)),
            pl.BlockSpec(everyone.shape, lambda g: (0, 0, 0)),
            pl.BlockSpec(spread.shape, lambda g: (0, 0, 0)),
        ],
        out_specs=pl.BlockSpec((2, 2, BS, HALF), lambda g: (0, g, 0, 0)),
        out_shape=jax.ShapeDtypeStruct((2, NBD, BS, HALF), jnp.bfloat16),
        scratch_shapes=[
            pltpu.VMEM((2, KB * 32 * GAP, 128), jnp.float32),
            pltpu.VMEM((NBD, 2 * NOCC, 128), jnp.bfloat16),
        ],
        compiler_params=pltpu.CompilerParams(vmem_limit_bytes=58 * MIB),
        cost_estimate=pl.CostEstimate(flops=2**30, bytes_accessed=20 * MIB, transcendentals=0),
    )(where, three_centre, everyone, spread)


def pack_kernel(jobs, n_in, index_ref, *refs):
    ins, outs, sems = refs[:n_in], refs[n_in:-1], refs[-1]
    copies = []
    for out, parts in zip(outs, jobs, strict=True):
        at = 0
        for source, row, first in parts:
            if row is None:
                copies.append((ins[source].at[pl.ds(first, NBD)], out.at[pl.ds(at, NBD)]))
                at += NBD
                continue
            for s in range(CAP):
                copies.append((ins[source].at[first + index_ref[row, s]], out.at[at + s]))
            at += CAP
    copies = [pltpu.make_async_copy(*copy, sems.at[n]) for n, copy in enumerate(copies)]
    for copy in copies:
        copy.start()
    for copy in copies:
        copy.wait()


def pack(jobs, sources, index, after):
    count = [sum(NBD if row is None else CAP for _, row, _ in parts) for parts in jobs]
    copies = sum(1 if row is None else CAP for parts in jobs for _, row, _ in parts)
    operands = [*sources, *after]
    return pl.pallas_call(
        functools.partial(pack_kernel, jobs, len(operands)),
        in_specs=[pl.BlockSpec(memory_space=pltpu.SMEM)]
        + [pl.BlockSpec(memory_space=pl.ANY)] * len(operands),
        out_specs=[pl.BlockSpec(memory_space=pltpu.VMEM)] * len(jobs),
        out_shape=[jax.ShapeDtypeStruct((n, BS, HALF), jnp.bfloat16) for n in count],
        scratch_shapes=[pltpu.SemaphoreType.DMA((copies,))],
        compiler_params=pltpu.CompilerParams(vmem_limit_bytes=58 * MIB),
        cost_estimate=pl.CostEstimate(flops=0, bytes_accessed=MIB, transcendentals=0),
    )(index, *operands)


def product_kernel(scale, jobs, per, n_in, split, index_ref, here_ref, own_ref, *refs):
    ins, outs = refs[:n_in], refs[n_in:-4]
    left, side, own_sems, sems = refs[-4:]
    step = pl.program_id(0)
    core = here_ref[1] & 1

    def own_copies():
        made = []
        for half in range(2):
            for n in range(FIT):
                piece = n
                if split:
                    piece = 2 * (n % (FIT // 2)) + (core if n < FIT // 2 else 1 - core)
                given = own_ref.at[half, pl.ds(pl.multiple_of(piece * PIECE, 32), PIECE)]
                made.append((given, left.at[half, pl.ds(n * PIECE, PIECE)], own_sems.at[half, n]))
        return [pltpu.make_async_copy(*copy) for copy in made]

    def copies(group, slot):
        made = []
        for n in range(per):
            for half, (source, row, first) in enumerate(jobs[group * per + n]):
                at = n * CAP
                if row is None:
                    given = ins[source].at[pl.ds(first, CAP)]
                    to = side.at[slot, half, pl.ds(at, CAP)]
                    made.append((given, to, sems.at[slot, half, at]))
                    continue
                for s in range(at, at + CAP):
                    given = ins[source].at[first + index_ref[row, s - at]]
                    made.append((given, side.at[slot, half, s], sems.at[slot, half, s]))
        return [pltpu.make_async_copy(*copy) for copy in made]

    def begin(job):
        for copy in copies(job, job % 2):
            copy.start()

    @pl.when(step == 0)
    def _():
        for copy in own_copies():
            copy.start()
        begin(0)
        for copy in own_copies():
            copy.wait()

    for job in range(len(jobs) // per):

        @pl.when(step == job)
        def _(job=job):
            if job + 1 < len(jobs) // per:
                begin(job + 1)
            for copy in copies(job, job % 2):
                copy.wait()

    slot = lax.rem(step, 2)
    last = (((1,), (1,)), ((), ()))
    side_a = side[slot, 0].reshape(per * CAP * BS, HALF)
    side_b = side[slot, 1].reshape(per * CAP * BS, HALF)
    total = lax.dot_general(left[0], side_a, last, preferred_element_type=jnp.float32)
    total += lax.dot_general(left[1], side_b, last, preferred_element_type=jnp.float32)
    total = (total * scale).astype(jnp.bfloat16)
    pieces = FIT // len(outs)
    for n in range(FIT):
        for t in range(per * TILES):
            part = total[n * PIECE : (n + 1) * PIECE, t * 128 : (t + 1) * 128]
            outs[n // pieces][n % pieces, t] = part


def product(
    own, jobs, sources, index, here, buffers, tile, count, scale, after, split, cost
):
    anywhere = pl.BlockSpec(memory_space=pl.ANY)
    smem = pl.BlockSpec(memory_space=pltpu.SMEM)
    extra = list(after) + list(buffers)
    given = [own.reshape(2, ROWS, HALF), *sources, *extra]
    operands = [index, here, *given]
    pieces = FIT // 2 if split else FIT
    shape = (pieces, count, PIECE, 128)
    kinds = [jnp.bfloat16] * (2 if split else 1)
    per = 2 if len(jobs) % 2 == 0 else 1
    block = per * TILES
    out = pl.BlockSpec((pieces, block, PIECE, 128), lambda j: (0, tile // block + j, 0, 0))
    return pl.pallas_call(
        functools.partial(product_kernel, scale, jobs, per, len(sources) + len(extra), split),
        grid=(len(jobs) // per,),
        in_specs=[smem, smem] + [anywhere] * len(given),
        out_specs=[out] * len(kinds),
        out_shape=[jax.ShapeDtypeStruct(shape, kind) for kind in kinds],
        scratch_shapes=[
            pltpu.VMEM((2, ROWS, HALF), jnp.bfloat16),
            pltpu.VMEM((2, 2, per * CAP, BS, HALF), jnp.bfloat16),
            pltpu.SemaphoreType.DMA((2, FIT)),
            pltpu.SemaphoreType.DMA((2, 2, per * CAP)),
        ],
        input_output_aliases={len(operands) - len(buffers) + n: n for n in range(len(buffers))},
        compiler_params=pltpu.CompilerParams(vmem_limit_bytes=58 * MIB),
        cost_estimate=pl.CostEstimate(flops=cost, bytes_accessed=MIB, transcendentals=0),
    )(*operands)


def add_kernel(here_ref, keep_ref, came_ref, own_ref, *send_refs):
    x = here_ref[1] >> 1
    own_ref[...] = keep_ref[x].astype(jnp.float32) + came_ref[x].astype(jnp.float32)
    for shift, send_ref in zip((2, 1, 3), send_refs, strict=True):
        there = (x + shift) & (SIDE - 1)
        value = keep_ref[there].astype(jnp.float32) + came_ref[there].astype(jnp.float32)
        send_ref[...] = value.astype(jnp.bfloat16)


def add_all_kernel(keep_ref, came_ref, out_ref):
    total = keep_ref[...].astype(jnp.float32) + came_ref[...].astype(jnp.float32)
    out_ref[...] = total.astype(jnp.bfloat16)


def add_cores_all(keep, came):
    block = pl.BlockSpec((FIT // 2, TILES, PIECE, 128), lambda j: (0, j, 0, 0))
    return pl.pallas_call(
        add_all_kernel,
        grid=(keep.shape[1] // TILES,),
        in_specs=[block, block],
        out_specs=block,
        out_shape=jax.ShapeDtypeStruct(keep.shape, jnp.bfloat16),
        compiler_params=pltpu.CompilerParams(vmem_limit_bytes=58 * MIB),
        cost_estimate=pl.CostEstimate(flops=0, bytes_accessed=MIB, transcendentals=0),
    )(keep, came)


def add_cores(here, keep, came):
    count = keep.shape[1]
    step = 5 if count % 5 == 0 else TILES
    block = pl.BlockSpec((FIT // 2, step, PIECE, 128), lambda j: (0, j, 0, 0))
    out = pl.BlockSpec((step, PIECE, 128), lambda j: (j, 0, 0))
    shape = (count, PIECE, 128)
    return pl.pallas_call(
        add_kernel,
        grid=(count // step,),
        in_specs=[pl.BlockSpec(memory_space=pltpu.SMEM), block, block],
        out_specs=[out] * 4,
        out_shape=[jax.ShapeDtypeStruct(shape, jnp.float32)]
        + [jax.ShapeDtypeStruct(shape, jnp.bfloat16)] * 3,
        compiler_params=pltpu.CompilerParams(vmem_limit_bytes=58 * MIB),
        cost_estimate=pl.CostEstimate(flops=0, bytes_accessed=MIB, transcendentals=0),
    )(here, keep, came)


def sum_kernel(given_ref, out_ref):
    value = given_ref[0].astype(jnp.float32)
    for n in range(1, given_ref.shape[0]):
        value += given_ref[n].astype(jnp.float32)
    out_ref[0] = value.astype(jnp.bfloat16)
    for t in range(TILES):
        out_ref[1, t] = pltpu.roll(value[t], 64, 1).astype(jnp.bfloat16)


def sum_pieces(given):
    count = given.shape[1]
    return pl.pallas_call(
        sum_kernel,
        grid=(count // TILES,),
        in_specs=[pl.BlockSpec((given.shape[0], TILES, PIECE, 128), lambda j: (0, j, 0, 0))],
        out_specs=pl.BlockSpec((2, TILES, PIECE, 128), lambda j: (0, j, 0, 0)),
        out_shape=jax.ShapeDtypeStruct((2, count, PIECE, 128), jnp.bfloat16),
        compiler_params=pltpu.CompilerParams(vmem_limit_bytes=58 * MIB),
        cost_estimate=pl.CostEstimate(flops=0, bytes_accessed=MIB, transcendentals=0),
    )(given)


def place_kernel(left_ref, right_ref, here_ref, *refs):
    parts, (out_ref, own, came, tiles, sems) = refs[:-5], refs[-5:]
    copies = []
    begin = 0
    for n, count in enumerate(COUNT[:2]):
        for turned in range(2):
            to = tiles.at[pl.ds(turned * (TOTAL + 1) + begin, count)]
            copies.append((parts[n].at[turned], to, sems.at[len(copies)]))
        begin += count
    copies.append((parts[2], own, sems.at[4]))
    copies += [(parts[3 + m], came.at[m], sems.at[5 + m]) for m in range(3)]
    copies = [pltpu.make_async_copy(*copy) for copy in copies]
    for copy in copies:
        copy.start()
    tiles[TOTAL] = jnp.zeros((PIECE, 128), jnp.bfloat16)
    for copy in copies:
        copy.wait()

    def add(tile, _):
        value = own[tile]
        for m in range(3):
            value += came[m, tile].astype(jnp.float32)
        tiles[begin + tile] = value.astype(jnp.bfloat16)
        tiles[TOTAL + 1 + begin + tile] = pltpu.roll(value, 64, 1).astype(jnp.bfloat16)
        return 0

    lax.fori_loop(0, COUNT[2], add, 0, unroll=3)
    is_left = lax.broadcasted_iota(jnp.int32, (PIECE, 128), 1) < 64

    def one(pair, _):
        value = jnp.where(is_left, tiles[left_ref[pair]], tiles[right_ref[pair]])
        out_ref[:, pl.ds(pl.multiple_of(pair * 128, 128), 128)] = value
        return 0

    lax.fori_loop(0, SIDE * SIDE * NBD // 2, one, 0, unroll=4)
    lane = lax.broadcasted_iota(jnp.int32, (PIECE, 128), 1)
    line = lax.broadcasted_iota(jnp.int32, (PIECE, 128), 0)
    row_block = (line + here_ref[1] * PIECE) >> 6
    for pair in range(NBD // 2):
        at = pl.ds(pl.multiple_of((here_ref[0] * (NBD // 2) + pair) * 128, 128), 128)
        value = out_ref[:, at].astype(jnp.float32)
        value = jnp.where(row_block == 2 * pair + (lane >> 6), 0.0, value)
        out_ref[:, at] = value.astype(jnp.bfloat16)


def place(source, here, parts):
    tile, odd = source >> 1, source & 1
    left = jnp.where(source < 0, TOTAL, jnp.where(odd == 0, tile, tile + TOTAL + 1))[0::2]
    right = jnp.where(source < 0, TOTAL, jnp.where(odd == 1, tile, tile + TOTAL + 1))[1::2]
    smem = pl.BlockSpec(memory_space=pltpu.SMEM)
    return pl.pallas_call(
        place_kernel,
        in_specs=[smem, smem, smem] + [pl.BlockSpec(memory_space=pl.ANY)] * len(parts),
        out_specs=pl.BlockSpec(memory_space=pltpu.VMEM),
        out_shape=jax.ShapeDtypeStruct((PIECE, SIDE * SIDE * NBD * BS), jnp.bfloat16),
        scratch_shapes=[
            pltpu.VMEM((COUNT[2], PIECE, 128), jnp.float32),
            pltpu.VMEM((3, COUNT[2], PIECE, 128), jnp.bfloat16),
            pltpu.VMEM((2 * TOTAL + 1, PIECE, 128), jnp.bfloat16),
            pltpu.SemaphoreType.DMA((8,)),
        ],
        compiler_params=pltpu.CompilerParams(vmem_limit_bytes=58 * MIB),
    )(left, right, here, *parts)


def per_device(three_centre, tensor_pattern, coefficients, readers):
    groups = SIDE * SIDE
    me = lax.axis_index("atom")
    lane = lax.axis_index("fit")
    everyone = jnp.broadcast_to(coefficients[None], (groups,) + coefficients.shape)
    everyone = lax.all_to_all(everyone, "atom", 0, 0, tiled=True)
    partner = tensor_pattern.reshape(-1)
    where = jnp.stack([partner // NBD, (partner % NBD) // 2, partner % 2]).astype(jnp.int32)
    own = fit_rows(three_centre, where, everyone)

    by_group = readers.reshape(groups, NBD, 4)
    pairs = jnp.asarray(PAIRS)[me]
    hit = jnp.any(by_group[pairs[:, 0]] == pairs[:, 1][:, None, None], axis=2)
    numbers = jnp.arange(NBD, dtype=jnp.int32)
    earlier = numbers[:, None] < numbers[None, :]
    rank = jnp.sum((hit[:, :, None] & earlier[None]).astype(jnp.int32), axis=1)
    slots = jnp.arange(CAP, dtype=jnp.int32)
    chosen = hit[:, None, :] & (rank[:, None, :] == slots[None, :, None])
    lists = jnp.sum(chosen.astype(jnp.int32) * numbers[None, None, :], axis=2)
    reads = jnp.any(by_group == me, axis=2)
    read_rank = jnp.sum((reads[:, :, None] & earlier[None]).astype(jnp.int32), axis=1)
    source = jnp.where(reads, 2 * jnp.asarray(BASE_OF)[me][:, None] + read_rank, -1)
    source = jnp.where(jnp.arange(groups)[:, None] == me, numbers[None, :], source).reshape(-1)

    scale = 1.0 / math.sqrt(FIT * 2 * HALF)
    def send(payload, step):
        route = [(number(a), number(plus(a, step))) for a in PLACES]
        return lax.ppermute(payload, "atom", route)

    here = jnp.stack([me, lane]).astype(jnp.int32)

    def multiply(jobs, buffers, tile, count, after, split=False, cost=0):
        sources = []
        for pair in jobs:
            for array, _, _ in pair:
                if not any(array is known for known in sources):
                    sources.append(array)
        at = lambda array: next(n for n, known in enumerate(sources) if known is array)
        jobs = tuple(tuple((at(array), row, first) for array, row, first in p) for p in jobs)
        return product(
            own, jobs, sources, lists, here, buffers, tile, count, scale, after, split, cost
        )

    def over_cores(to_send):
        return lax.ppermute(to_send, "fit", [(n, n ^ 1) for n in range(FIT)])

    def over_chips(pieces):
        sent = []
        for shift, piece in zip((2, 1, 3), pieces, strict=True):
            route = [(n, (n + 2 * shift) % FIT) for n in range(FIT)]
            sent.append(lax.ppermute(piece, "fit", route))
        return sent

    def exchange(pieces):
        groups = [list(range(core, FIT, 2)) for core in range(2)]
        return lax.all_to_all(pieces, "fit", 0, 0, axis_index_groups=groups, tiled=True)

    def leaf_row(o):
        return len(WHOLE) + [p[0] for p in LEAVES].index(o)

    def both(source, row):
        return ((source, row, 0), (source, row, NBD))

    def hop(leaf):
        return minus(*leaf)

    own = own.reshape(2 * NBD, BS, HALF)
    near = [send(own, o) for o in NEAR]
    jobs = [[(own, None, half * NBD + part * CAP) for half in range(2)] for part in range(2)]
    partial = multiply(jobs, [], 0, COUNT[0], [], True)
    jobs = []
    for n, (o, sender) in enumerate(CORNERS):
        jobs.append(((n, None, (n % 2) * NBD), *both(NEAR.index(sender), leaf_row(o))))
    packed = pack(tuple(jobs), near, lists, partial[:1])
    second = [send(packed[n], o) for n, o in enumerate(NEAR)]
    jobs = [[(near[n], n, 0), (near[n], n, NBD)] for n in range(4)]
    keep, to_send = multiply(jobs, partial, OWN_TILES, COUNT[0], packed[:1], True)
    first_pieces = add_cores_all(keep, over_cores(to_send))
    jobs = []
    for o, sender in EDGES:
        m, row = 2 * MIDDLE.index(sender), leaf_row(o)
        jobs.append(((m, row, 0), (m + 1, row, 0)))
    jobs.append(((0, leaf_row((2, 2)), 0),))
    packed = pack(tuple(jobs), second, lists, [first_pieces])
    last = [send(packed[4], hop(FAR[0]))]
    third = [send(packed[n], hop(leaf)) for n, leaf in enumerate(EDGES)]
    first_came = exchange(first_pieces)
    jobs = [[(second[2 * m], 4 + m, 0), (second[2 * m + 1], 4 + m, 0)] for m in range(2)]
    jobs += [[(second[n], None, NBD), (second[n], None, NBD + CAP)] for n in range(4)]
    (partial,) = multiply(jobs, [], 0, COUNT[1], packed[:1])
    second_came = lax.all_to_all(partial, "fit", 0, 0, tiled=True)
    jobs = (((0, leaf_row((2, 2)) + 1, 0),),)
    last.append(send(pack(jobs, second[3:], lists, [partial])[0], hop(FAR[1])))
    jobs = [[(array, None, 0), (array, None, CAP)] for array in third]
    jobs.append([(array, None, 0) for array in last])
    keep, to_send = multiply(jobs, [], 0, COUNT[2], [first_came], True, 10**12)
    pieces = add_cores(here, keep, over_cores(to_send))
    third_came = over_chips(pieces[1:])
    parts = [sum_pieces(first_came), sum_pieces(second_came), pieces[0], *third_came]
    return place(source, here, parts)


def solution(mesh):
    placed = (P("atom", None, "fit", None), P("atom", None), P(None, "atom"), P())
    return jax.shard_map(
        per_device, mesh=mesh, in_specs=placed, out_specs=P(("atom", "fit"), None), check_vma=False
    )
```
